32 devices in a mesh: group: 2 (over x), blk: 16 (over z, y, core).
Axes of the slice: x: 2, y: 2, z: 4, core: 2. Of those that a mesh axis runs over, the one named last changes fastest.
Arguments:
- wavefunction: bfloat16 [256, 3, 128, 128], P(('group', 'blk')), parts along dimension 0, may hold values from -6 to 6
- left_operators: bfloat16 [256, 16, 128, 128], P(('group', 'blk')), parts along dimension 0, may hold values from -0.5 to 0.5
- right_operators: bfloat16 [4096, 128, 128], P(('group', 'blk')), parts along dimension 0, may hold values from -0.5 to 0.5
- shifts: int32 [32], P('group'), parts along dimension 0, may hold values from -1 to 1
- term_mask: int32 [256, 16], P(('group', 'blk')), parts along dimension 0, may hold values 0 or 1
- slot_table: int32 [256, 16], P(('group', 'blk')), parts along dimension 0, may hold values from 0 to 127, as said below
Outputs:
- product_vectors: bfloat16 [256, 3, 128, 128], P(('group', 'blk')), parts along dimension 0
The draws below stay inside these ranges and needn't reach their ends.
There are 2 independent parts, one for each index of `group`. The reference program is written for one: setup_inputs(seed, part) draws one part's arguments, and reference() takes and returns one part's arrays. A program takes and returns all parts, laid end to end along the dimension named above; each array names one. Nothing has to cross between parts.
Inputs may be any that keep to these rules, and one draw needn't show every extreme that they name: `slot_table`: for the 8 blocks of one device, the 128 entries are a permutation of 0 to 127, so every device owns exactly 8 right operator for each device's blocks.
All inputs are finite; a program needn't handle non-finite values. No bound on the sum of `term_mask` on one device may be relied on, other than what follows from the above.
Results may differ from the reference program's by a relative error of at most 0.008.
Values may be sent and summed in bfloat16 or wider, within the bound.
A program may use at most 128 MiB of HBM per device.

```python
import jax
import jax.numpy as jnp
from jax import lax

DIM = 128
NT = 16
NVEC = 3
BLK_DEV = 8
NB = 128
N_BLK = 16


def permute_items(subkey):
    return jax.random.permutation(subkey, BLK_DEV * NT)


def draw_slot_table(key, part):
    key = jax.random.fold_in(key, 7)
    sources = NB // BLK_DEV
    subkeys = jax.random.split(key, sources)
    orders = jax.vmap(permute_items)(subkeys)
    return orders.reshape(NB, NT).astype(jnp.int32)


def set_ends(entries, key, low, high):
    place = [jax.random.randint(jax.random.fold_in(key, axis), (), 0, length) for axis, length in enumerate(entries.shape)]
    main_axis = entries.shape.index(max(entries.shape))
    beside = place[:main_axis] + [(place[main_axis] + 1) % entries.shape[main_axis]] + place[main_axis + 1:]
    return entries.at[tuple(place)].set(low).at[tuple(beside)].set(high)


def block_scale(key, shape, cuts, smallest, high):
    level, own = 1.0, jax.random.fold_in(key, 6)
    for dim, shards_of in cuts:
        steps = jnp.exp(jax.random.uniform(jax.random.fold_in(own, dim), (shards_of,), jnp.float32, smallest / len(cuts), high / len(cuts)))
        level = level * jnp.repeat(steps, shape[dim] // shards_of).reshape([-1 if axis == dim else 1 for axis in range(len(shape))])
    return level


def noise(key, extent, scale, limit, shards=(), held_as=jnp.bfloat16):
    factor_of = block_scale(key, extent, shards, -0.22, 0.18) if shards else 1.0
    entries = jax.random.normal(key, extent, jnp.float32) * scale * factor_of
    return jnp.minimum(jnp.maximum(entries, -limit), limit).astype(held_as)


def setup_inputs(seed: int = 0, part: int = 0) -> dict:
    seeds = jax.random.split(jax.random.key(seed), 7)
    part_keys = jax.random.split(jax.random.fold_in(seeds[6], part), 7)
    return {
        "wavefunction": noise(part_keys[0], (NB, NVEC, DIM, DIM), 1.0, 6.0, ((0, 16),)),
        "left_operators": noise(part_keys[1], (NB, NT, DIM, DIM), DIM ** -0.5, 0.5, ((0, 16),)),
        "right_operators": noise(part_keys[2], (NB * NT, DIM, DIM), DIM ** -0.5, 0.5, ((0, 16),)),
        "shifts": set_ends(jax.random.randint(part_keys[3], (NT,), -1, 2), jax.random.fold_in(part_keys[3], 1), -1, 1).astype(jnp.int32),
        "term_mask": set_ends((jax.random.randint(part_keys[4], (NB, NT), 0, 4) < 3).astype(jnp.int32), jax.random.fold_in(part_keys[4], 1), 0, 1),
        "slot_table": draw_slot_table(jax.random.fold_in(jax.random.fold_in(seeds[6], part), 71), part),
    }


def reference(wavefunction, left_operators, right_operators, shifts, term_mask, slot_table):
    zero_block = jnp.zeros((1, NVEC, DIM, DIM), jnp.bfloat16)
    padded = jnp.concatenate([zero_block, wavefunction, zero_block], axis=0)
    item_count = BLK_DEV * NT
    per_peer = item_count // N_BLK
    source = (jnp.arange(NB, dtype=jnp.int32) // BLK_DEV)[:, None]
    owner_device = slot_table // per_peer
    within = slot_table % per_peer
    right_rows = (owner_device * item_count + source * per_peer + within).astype(jnp.int32)

    def per_block(block):
        source_rows = (block + 1 - shifts).astype(jnp.int32)
        pieces = jnp.take(padded, source_rows, axis=0)
        left_block = jnp.take(left_operators, block, axis=0)
        left_done = jnp.einsum('txy,tvyz->tvxz', left_block.astype(jnp.float32), pieces.astype(jnp.float32))
        weights = jnp.take(term_mask, block, axis=0).astype(jnp.float32)
        left_done = (left_done * weights[:, None, None, None]).astype(jnp.bfloat16)
        right_block = jnp.take(right_operators, jnp.take(right_rows, block, axis=0), axis=0)
        term_blocks = jnp.einsum('tvxy,tzy->tvxz', left_done.astype(jnp.float32), right_block.astype(jnp.float32)).astype(jnp.bfloat16)
        return jnp.sum(term_blocks.astype(jnp.float32), axis=0).astype(jnp.bfloat16)

    return lax.map(per_block, jnp.arange(NB, dtype=jnp.int32))
```

```python
import functools

import jax
import jax.numpy as jnp
from jax import lax
from jax.experimental import pallas as pl
from jax.experimental.pallas import tpu as pltpu
from jax.sharding import PartitionSpec as P

MESH = pl.DeviceIdType.MESH
PIECES = 1


def partner(me, k, n):
    out = 0
    bit = 1
    while bit < n:
        out = out + bit * ((me // bit + k // bit) % 2)
        bit *= 2
    return out


def offset_of(step, n):
    odd = step % 2
    return (1 - odd) * (n // 2 + step // 2) + odd * ((step + 1) // 2)


def kernel(
    n, pieces, shifts, mask, slots, slots_v, wave, left, right, out,
    wpad, left_v, done, recv, terms, inverse,
    local_sem, left_sem, halo_send, halo_recv, send_sem, recv_sem,
):
    me = lax.axis_index("blk")
    blocks, term_count = left.shape[0], left.shape[1]
    vectors, width = wave.shape[1], wave.shape[2]
    items = blocks * term_count
    per = items // n
    size = per // pieces
    last = n - 1

    barrier = pltpu.get_barrier_semaphore()

    @pl.loop(1, n)
    def _(k):
        pl.semaphore_signal(
            barrier, inc=1, device_id={"blk": partner(me, k, n)}, device_id_type=MESH
        )

    wave_copy = pltpu.make_async_copy(wave, wpad.at[pl.ds(1, blocks)], local_sem.at[0])
    wave_copy.start()
    own = pl.ds(me * per, per)
    own_copy = pltpu.make_async_copy(right.at[own], recv.at[own], local_sem.at[1])
    own_copy.start()
    left_copies = [
        pltpu.make_async_copy(left.at[a], left_v.at[a], left_sem.at[a]) for a in range(blocks)
    ]
    for copy in left_copies:
        copy.start()

    pl.semaphore_wait(barrier, n - 1)

    def halo(up):
        return pltpu.make_async_remote_copy(
            src_ref=wave.at[blocks - 1 if up else 0],
            dst_ref=wpad.at[0 if up else blocks + 1],
            send_sem=halo_send.at[1 if up else 0],
            recv_sem=halo_recv.at[1 if up else 0],
            device_id={"blk": (me + 1) % n if up else (me + n - 1) % n},
            device_id_type=MESH,
        )

    @pl.when(me < last)
    def _():
        halo(True).start()

    @pl.when(me > 0)
    def _():
        halo(False).start()

    def sending(step, piece):
        peer = partner(me, offset_of(step, n), n)
        return pltpu.make_async_remote_copy(
            src_ref=right.at[pl.ds(peer * per + piece * size, size)],
            dst_ref=recv.at[pl.ds(me * per + piece * size, size)],
            send_sem=send_sem.at[piece, step],
            recv_sem=recv_sem.at[piece, step],
            device_id={"blk": peer},
            device_id_type=MESH,
        )

    def arriving(step, piece):
        peer = partner(me, offset_of(step, n), n)
        here = recv.at[pl.ds(peer * per + piece * size, size)]
        return pltpu.make_async_remote_copy(
            src_ref=here,
            dst_ref=here,
            send_sem=send_sem.at[piece, step],
            recv_sem=recv_sem.at[piece, step],
            device_id={"blk": peer},
            device_id_type=MESH,
        )

    for piece in range(pieces):

        @pl.loop(0, n - 1)
        def _(step, piece=piece):
            sending(step, piece).start()

    table = slots_v[...]
    place = lax.broadcasted_iota(jnp.int32, table.shape, 0) * term_count + lax.broadcasted_iota(
        jnp.int32, table.shape, 1
    )

    @pl.loop(0, items)
    def _(s):
        inverse[s] = jnp.max(jnp.where(table == s, place, 0))

    wave_copy.wait()

    @pl.when(me < last)
    def _():
        halo(True).wait_send()
        halo(False).wait_recv()

    @pl.when(me > 0)
    def _():
        halo(False).wait_send()
        halo(True).wait_recv()

    @pl.when(me == 0)
    def _():
        wpad[0] = jnp.zeros(wpad.shape[1:], wpad.dtype)

    @pl.when(me == last)
    def _():
        wpad[blocks + 1] = jnp.zeros(wpad.shape[1:], wpad.dtype)

    for copy in left_copies:
        copy.wait()

    @pl.loop(0, blocks)
    def _(a):
        @pl.loop(0, term_count)
        def _(t):
            row = a + 1 - shifts[t]
            piece = wpad[row]
            beside = jnp.concatenate([piece[v] for v in range(vectors)], axis=1)
            product = jnp.dot(left_v[a, t], beside, preferred_element_type=jnp.float32)
            product = (product * mask[a, t].astype(jnp.float32)).astype(jnp.bfloat16)
            for v in range(vectors):
                done[a * term_count + t, pl.ds(v * width, width)] = product[
                    :, v * width : (v + 1) * width
                ]

    def multiply(first, count):
        for j in range(count):
            s = first + j
            terms[s] = lax.dot_general(
                done[inverse[s]],
                recv[s],
                (((1,), (1,)), ((), ())),
                preferred_element_type=jnp.float32,
            ).astype(jnp.bfloat16)

    own_copy.wait()
    multiply(me * per, per)
    for piece in range(pieces):

        @pl.loop(0, n - 1)
        def _(step, piece=piece):
            arriving(step, piece).wait_recv()
            multiply(partner(me, offset_of(step, n), n) * per + piece * size, size)

    @pl.loop(0, blocks)
    def _(a):
        for v in range(vectors):
            total = jnp.zeros((width, width), jnp.float32)
            for t in range(term_count):
                total += terms[slots[a, t], pl.ds(v * width, width)].astype(jnp.float32)
            out[a, v] = total.astype(out.dtype)

    for piece in range(pieces):

        @pl.loop(0, n - 1)
        def _(step, piece=piece):
            sending(step, piece).wait_send()


def per_device(wavefunction, left_operators, right_operators, shifts, term_mask, slot_table):
    n = lax.axis_size("blk")
    blocks, vectors, width = wavefunction.shape[:3]
    term_count = left_operators.shape[1]
    items = blocks * term_count
    per = items // n
    pieces = PIECES if per % PIECES == 0 else 1
    smem = pl.BlockSpec(memory_space=pltpu.SMEM)
    vmem = pl.BlockSpec(memory_space=pltpu.VMEM)
    hbm = pl.BlockSpec(memory_space=pl.ANY)
    dma = pltpu.SemaphoreType.DMA
    return pl.pallas_call(
        functools.partial(kernel, n, pieces),
        out_shape=jax.ShapeDtypeStruct(wavefunction.shape, jnp.bfloat16),
        in_specs=[smem, smem, smem, vmem, hbm, hbm, hbm],
        out_specs=vmem,
        scratch_shapes=[
            pltpu.VMEM((blocks + 2, vectors, width, width), jnp.bfloat16),
            pltpu.VMEM((blocks, term_count, width, width), jnp.bfloat16),
            pltpu.VMEM((items, vectors * width, width), jnp.bfloat16),
            pltpu.VMEM((items, width, width), jnp.bfloat16),
            pltpu.VMEM((items, vectors * width, width), jnp.bfloat16),
            pltpu.SMEM((items,), jnp.int32),
            dma((2,)),
            dma((blocks,)),
            dma((2,)),
            dma((2,)),
            dma((pieces, n - 1)),
            dma((pieces, n - 1)),
        ],
        compiler_params=pltpu.CompilerParams(
            collective_id=0, has_side_effects=True, vmem_limit_bytes=52 * 1024 * 1024
        ),
        cost_estimate=pl.CostEstimate(
            flops=4 * items * vectors * width**3,
            bytes_accessed=4 * items * width * width,
            transcendentals=0,
        ),
        name="sector_product",
    )(shifts, term_mask, slot_table, slot_table, wavefunction, left_operators, right_operators)


def solution(mesh):
    placed = (
        P(("group", "blk"), None, None, None),
        P(("group", "blk"), None, None, None),
        P(("group", "blk"), None, None),
        P("group"),
        P(("group", "blk"), None),
        P(("group", "blk"), None),
    )
    return jax.shard_map(
        per_device,
        mesh=mesh,
        in_specs=placed,
        out_specs=P(("group", "blk"), None, None, None),
        check_vma=False,
    )
```

```python
import functools

import jax
import jax.numpy as jnp
from jax import lax
from jax.experimental import pallas as pl
from jax.experimental.pallas import tpu as pltpu
from jax.sharding import PartitionSpec as P

MESH = pl.DeviceIdType.MESH
PIECES = 1


def partner(me, k, n):
    out = 0
    bit = 1
    while bit < n:
        out = out + bit * ((me // bit + k // bit) % 2)
        bit *= 2
    return out


def offset_of(step, n):
    odd = step % 2
    return (1 - odd) * (n // 2 + step // 2) + odd * ((step + 1) // 2)


def kernel(
    n, pieces, shifts_in, mask_in, slots_in, wave, left, right, out,
    shifts, mask, slots, slots_v, wpad, left_v, done, recv, terms, inverse,
    local_sem, table_sem, left_sem, halo_send, halo_recv, send_sem, recv_sem,
):
    me = lax.axis_index("blk")
    blocks, term_count = left.shape[0], left.shape[1]
    vectors, width = wave.shape[1], wave.shape[2]
    items = blocks * term_count
    per = items // n
    size = per // pieces
    last = n - 1

    barrier = pltpu.get_barrier_semaphore()

    @pl.loop(1, n)
    def _(k):
        pl.semaphore_signal(
            barrier, inc=1, device_id={"blk": partner(me, k, n)}, device_id_type=MESH
        )

    table_copies = [
        pltpu.make_async_copy(source, target, table_sem.at[i])
        for i, (source, target) in enumerate(
            ((shifts_in, shifts), (mask_in, mask), (slots_in, slots), (slots_in, slots_v))
        )
    ]
    for copy in table_copies:
        copy.start()
    wave_copy = pltpu.make_async_copy(wave, wpad.at[pl.ds(1, blocks)], local_sem.at[0])
    wave_copy.start()
    own = pl.ds(me * per, per)
    own_copy = pltpu.make_async_copy(right.at[own], recv.at[own], local_sem.at[1])
    own_copy.start()
    left_copies = [
        pltpu.make_async_copy(left.at[a], left_v.at[a], left_sem.at[a]) for a in range(blocks)
    ]
    for copy in left_copies:
        copy.start()

    pl.semaphore_wait(barrier, n - 1)

    def halo(up):
        return pltpu.make_async_remote_copy(
            src_ref=wave.at[blocks - 1 if up else 0],
            dst_ref=wpad.at[0 if up else blocks + 1],
            send_sem=halo_send.at[1 if up else 0],
            recv_sem=halo_recv.at[1 if up else 0],
            device_id={"blk": (me + 1) % n if up else (me + n - 1) % n},
            device_id_type=MESH,
        )

    @pl.when(me < last)
    def _():
        halo(True).start()

    @pl.when(me > 0)
    def _():
        halo(False).start()

    def sending(step, piece):
        peer = partner(me, offset_of(step, n), n)
        return pltpu.make_async_remote_copy(
            src_ref=right.at[pl.ds(peer * per + piece * size, size)],
            dst_ref=recv.at[pl.ds(me * per + piece * size, size)],
            send_sem=send_sem.at[piece, step],
            recv_sem=recv_sem.at[piece, step],
            device_id={"blk": peer},
            device_id_type=MESH,
        )

    def arriving(step, piece):
        peer = partner(me, offset_of(step, n), n)
        here = recv.at[pl.ds(peer * per + piece * size, size)]
        return pltpu.make_async_remote_copy(
            src_ref=here,
            dst_ref=here,
            send_sem=send_sem.at[piece, step],
            recv_sem=recv_sem.at[piece, step],
            device_id={"blk": peer},
            device_id_type=MESH,
        )

    for piece in range(pieces):

        @pl.loop(0, n - 1)
        def _(step, piece=piece):
            sending(step, piece).start()

    for copy in table_copies:
        copy.wait()

    table = slots_v[...]
    place = lax.broadcasted_iota(jnp.int32, table.shape, 0) * term_count + lax.broadcasted_iota(
        jnp.int32, table.shape, 1
    )

    @pl.loop(0, items)
    def _(s):
        inverse[s] = jnp.max(jnp.where(table == s, place, 0))

    wave_copy.wait()

    @pl.when(me < last)
    def _():
        halo(True).wait_send()
        halo(False).wait_recv()

    @pl.when(me > 0)
    def _():
        halo(False).wait_send()
        halo(True).wait_recv()

    @pl.when(me == 0)
    def _():
        wpad[0] = jnp.zeros(wpad.shape[1:], wpad.dtype)

    @pl.when(me == last)
    def _():
        wpad[blocks + 1] = jnp.zeros(wpad.shape[1:], wpad.dtype)

    for copy in left_copies:
        copy.wait()

    @pl.loop(0, blocks)
    def _(a):
        @pl.loop(0, term_count)
        def _(t):
            row = a + 1 - shifts[t]
            piece = wpad[row]
            beside = jnp.concatenate([piece[v] for v in range(vectors)], axis=1)
            product = jnp.dot(left_v[a, t], beside, preferred_element_type=jnp.float32)
            product = (product * mask[a, t].astype(jnp.float32)).astype(jnp.bfloat16)
            for v in range(vectors):
                done[a * term_count + t, pl.ds(v * width, width)] = product[
                    :, v * width : (v + 1) * width
                ]

    def multiply(first, count):
        for j in range(count):
            s = first + j
            terms[s] = lax.dot_general(
                done[inverse[s]],
                recv[s],
                (((1,), (1,)), ((), ())),
                preferred_element_type=jnp.float32,
            ).astype(jnp.bfloat16)

    own_copy.wait()
    multiply(me * per, per)
    for piece in range(pieces):

        @pl.loop(0, n - 1)
        def _(step, piece=piece):
            arriving(step, piece).wait_recv()
            multiply(partner(me, offset_of(step, n), n) * per + piece * size, size)

    @pl.loop(0, blocks)
    def _(a):
        for v in range(vectors):
            total = jnp.zeros((width, width), jnp.float32)
            for t in range(term_count):
                total += terms[slots[a, t], pl.ds(v * width, width)].astype(jnp.float32)
            out[a, v] = total.astype(out.dtype)

    for piece in range(pieces):

        @pl.loop(0, n - 1)
        def _(step, piece=piece):
            sending(step, piece).wait_send()


def per_device(wavefunction, left_operators, right_operators, shifts, term_mask, slot_table):
    n = lax.axis_size("blk")
    blocks, vectors, width = wavefunction.shape[:3]
    term_count = left_operators.shape[1]
    items = blocks * term_count
    per = items // n
    pieces = PIECES if per % PIECES == 0 else 1
    hbm = pl.BlockSpec(memory_space=pltpu.HBM)
    dma = pltpu.SemaphoreType.DMA
    return pl.pallas_call(
        functools.partial(kernel, n, pieces),
        out_shape=jax.ShapeDtypeStruct(wavefunction.shape, jnp.bfloat16),
        in_specs=[hbm] * 6,
        out_specs=pl.BlockSpec(memory_space=pltpu.VMEM),
        scratch_shapes=[
            pltpu.SMEM(shifts.shape, jnp.int32),
            pltpu.SMEM(term_mask.shape, jnp.int32),
            pltpu.SMEM(slot_table.shape, jnp.int32),
            pltpu.VMEM(slot_table.shape, jnp.int32),
            pltpu.VMEM((blocks + 2, vectors, width, width), jnp.bfloat16),
            pltpu.VMEM((blocks, term_count, width, width), jnp.bfloat16),
            pltpu.VMEM((items, vectors * width, width), jnp.bfloat16),
            pltpu.VMEM((items, width, width), jnp.bfloat16),
            pltpu.VMEM((items, vectors * width, width), jnp.bfloat16),
            pltpu.SMEM((items,), jnp.int32),
            dma((2,)),
            dma((4,)),
            dma((blocks,)),
            dma((2,)),
            dma((2,)),
            dma((pieces, n - 1)),
            dma((pieces, n - 1)),
        ],
        compiler_params=pltpu.CompilerParams(
            collective_id=0, has_side_effects=True, vmem_limit_bytes=52 * 1024 * 1024
        ),
        cost_estimate=pl.CostEstimate(
            flops=4 * items * vectors * width**3,
            bytes_accessed=4 * items * width * width,
            transcendentals=0,
        ),
        name="sector_product",
    )(shifts, term_mask, slot_table, wavefunction, left_operators, right_operators)


def solution(mesh):
    placed = (
        P(("group", "blk"), None, None, None),
        P(("group", "blk"), None, None, None),
        P(("group", "blk"), None, None),
        P("group"),
        P(("group", "blk"), None),
        P(("group", "blk"), None),
    )
    return jax.shard_map(
        per_device,
        mesh=mesh,
        in_specs=placed,
        out_specs=P(("group", "blk"), None, None, None),
        check_vma=False,
    )
```

```python
import functools

import jax
import jax.numpy as jnp
from jax import lax
from jax.experimental import pallas as pl
from jax.experimental.pallas import tpu as pltpu
from jax.sharding import PartitionSpec as P

MESH = pl.DeviceIdType.MESH
VMEM_LIMIT = 54 * 1024 * 1024


def partner(me, k, n):
    out = 0
    bit = 1
    while bit < n:
        out = out + bit * ((me // bit + k // bit) % 2)
        bit *= 2
    return out


def offset_of(step, n):
    odd = step % 2
    return (1 - odd) * (n // 2 + step // 2) + odd * ((step + 1) // 2)


def kernel(
    n, shifts_in, mask_in, slots_in, wave, left, right, out,
    shifts, mask, slots, slots_v, wpad, left_v, done, recv, sums, item_of, sum_before,
    local_sem, table_sem, left_sem, halo_send, halo_recv, send_sem, recv_sem,
):
    me = lax.axis_index("blk")
    blocks, term_count = left.shape[0], left.shape[1]
    vectors, width = wave.shape[1], wave.shape[2]
    items = blocks * term_count
    per = items // n
    last = n - 1

    barrier = pltpu.get_barrier_semaphore()

    @pl.loop(1, n)
    def _(k):
        pl.semaphore_signal(
            barrier, inc=1, device_id={"blk": partner(me, k, n)}, device_id_type=MESH
        )

    table_copies = [
        pltpu.make_async_copy(source, target, table_sem.at[i])
        for i, (source, target) in enumerate(
            ((shifts_in, shifts), (mask_in, mask), (slots_in, slots), (slots_in, slots_v))
        )
    ]
    for copy in table_copies:
        copy.start()
    wave_copy = pltpu.make_async_copy(wave, wpad.at[pl.ds(1, blocks)], local_sem.at[0])
    wave_copy.start()
    own = pl.ds(me * per, per)
    own_copy = pltpu.make_async_copy(right.at[own], recv.at[own], local_sem.at[1])
    own_copy.start()
    left_copies = [
        pltpu.make_async_copy(left.at[a], left_v.at[a], left_sem.at[a]) for a in range(blocks)
    ]
    for copy in left_copies:
        copy.start()

    pl.semaphore_wait(barrier, n - 1)

    def halo(up):
        return pltpu.make_async_remote_copy(
            src_ref=wave.at[blocks - 1 if up else 0],
            dst_ref=wpad.at[0 if up else blocks + 1],
            send_sem=halo_send.at[1 if up else 0],
            recv_sem=halo_recv.at[1 if up else 0],
            device_id={"blk": (me + 1) % n if up else (me + n - 1) % n},
            device_id_type=MESH,
        )

    @pl.when(me < last)
    def _():
        halo(True).start()

    @pl.when(me > 0)
    def _():
        halo(False).start()

    def sending(step):
        peer = partner(me, offset_of(step, n), n)
        return pltpu.make_async_remote_copy(
            src_ref=right.at[pl.ds(peer * per, per)],
            dst_ref=recv.at[pl.ds(me * per, per)],
            send_sem=send_sem.at[step],
            recv_sem=recv_sem.at[step],
            device_id={"blk": peer},
            device_id_type=MESH,
        )

    def arriving(step):
        peer = partner(me, offset_of(step, n), n)
        here = recv.at[pl.ds(peer * per, per)]
        return pltpu.make_async_remote_copy(
            src_ref=here,
            dst_ref=here,
            send_sem=send_sem.at[step],
            recv_sem=recv_sem.at[step],
            device_id={"blk": peer},
            device_id_type=MESH,
        )

    @pl.loop(0, n - 1)
    def _(step):
        sending(step).start()

    for copy in table_copies:
        copy.wait()

    table = slots_v[...]
    place = lax.broadcasted_iota(jnp.int32, table.shape, 0) * term_count + lax.broadcasted_iota(
        jnp.int32, table.shape, 1
    )
    offset = partner(me, table // per, n)
    rank = jnp.where(
        offset == 0, 0, jnp.where(offset >= n // 2, 2 * offset - n + 1, 2 * offset)
    )
    position = rank * per + table % per

    def look_up(p, latest):
        here = position == p
        row = jnp.max(here.astype(jnp.int32), axis=1, keepdims=True)
        item_of[p] = jnp.max(jnp.where(here, place, 0))
        sum_before[p] = jnp.max(row * latest)
        return jnp.where(row > 0, p + 1, latest)

    latest = lax.fori_loop(0, items, look_up, jnp.zeros((blocks, 1), jnp.int32))
    rows = lax.broadcasted_iota(jnp.int32, (blocks, 1), 0)
    for a in range(blocks):
        sum_before[items + a] = jnp.max(jnp.where(rows == a, latest, 0))
    sums[0] = jnp.zeros(sums.shape[1:], sums.dtype)

    wave_copy.wait()

    @pl.when(me < last)
    def _():
        halo(True).wait_send()
        halo(False).wait_recv()

    @pl.when(me > 0)
    def _():
        halo(False).wait_send()
        halo(True).wait_recv()

    @pl.when(me == 0)
    def _():
        wpad[0] = jnp.zeros(wpad.shape[1:], wpad.dtype)

    @pl.when(me == last)
    def _():
        wpad[blocks + 1] = jnp.zeros(wpad.shape[1:], wpad.dtype)

    for copy in left_copies:
        copy.wait()

    @pl.loop(0, blocks)
    def _(a):
        @pl.loop(0, term_count)
        def _(t):
            row = a + 1 - shifts[t]
            piece = wpad[row]
            beside = jnp.concatenate([piece[v] for v in range(vectors)], axis=1)
            product = jnp.dot(left_v[a, t], beside, preferred_element_type=jnp.float32)
            product = (product * mask[a, t].astype(jnp.float32)).astype(jnp.bfloat16)
            for v in range(vectors):
                done[a * term_count + t, pl.ds(v * width, width)] = product[
                    :, v * width : (v + 1) * width
                ]

    def multiply(place, first):
        for j in range(per):
            term = lax.dot_general(
                done[item_of[place + j]],
                recv[first + j],
                (((1,), (1,)), ((), ())),
                preferred_element_type=jnp.float32,
            ).astype(jnp.bfloat16)
            sums[place + j + 1] = sums[sum_before[place + j]] + term.astype(jnp.float32)

    own_copy.wait()
    multiply(0, me * per)
    @pl.loop(0, n - 1)
    def _(step):
        arriving(step).wait_recv()
        multiply((step + 1) * per, partner(me, offset_of(step, n), n) * per)

    @pl.loop(0, blocks)
    def _(a):
        total = sums[sum_before[items + a]]
        for v in range(vectors):
            out[a, v] = total[v * width : (v + 1) * width].astype(out.dtype)

    @pl.loop(0, n - 1)
    def _(step):
        sending(step).wait_send()


def per_device(wavefunction, left_operators, right_operators, shifts, term_mask, slot_table):
    n = lax.axis_size("blk")
    blocks, vectors, width = wavefunction.shape[:3]
    term_count = left_operators.shape[1]
    items = blocks * term_count
    per = items // n
    hbm = pl.BlockSpec(memory_space=pltpu.HBM)
    dma = pltpu.SemaphoreType.DMA
    return pl.pallas_call(
        functools.partial(kernel, n),
        out_shape=jax.ShapeDtypeStruct(wavefunction.shape, jnp.bfloat16),
        in_specs=[hbm] * 6,
        out_specs=pl.BlockSpec(memory_space=pltpu.VMEM),
        scratch_shapes=[
            pltpu.SMEM(shifts.shape, jnp.int32),
            pltpu.SMEM(term_mask.shape, jnp.int32),
            pltpu.SMEM(slot_table.shape, jnp.int32),
            pltpu.VMEM(slot_table.shape, jnp.int32),
            pltpu.VMEM((blocks + 2, vectors, width, width), jnp.bfloat16),
            pltpu.VMEM((blocks, term_count, width, width), jnp.bfloat16),
            pltpu.VMEM((items, vectors * width, width), jnp.bfloat16),
            pltpu.VMEM((items, width, width), jnp.bfloat16),
            pltpu.VMEM((items + 1, vectors * width, width), jnp.float32),
            pltpu.SMEM((items,), jnp.int32),
            pltpu.SMEM((items + blocks,), jnp.int32),
            dma((2,)),
            dma((4,)),
            dma((blocks,)),
            dma((2,)),
            dma((2,)),
            dma((n - 1,)),
            dma((n - 1,)),
        ],
        compiler_params=pltpu.CompilerParams(
            collective_id=0, has_side_effects=True, vmem_limit_bytes=VMEM_LIMIT
        ),
        cost_estimate=pl.CostEstimate(
            flops=4 * items * vectors * width**3,
            bytes_accessed=4 * items * width * width,
            transcendentals=0,
        ),
        name="sector_product",
    )(shifts, term_mask, slot_table, wavefunction, left_operators, right_operators)


def solution(mesh):
    placed = (
        P(("group", "blk"), None, None, None),
        P(("group", "blk"), None, None, None),
        P(("group", "blk"), None, None),
        P("group"),
        P(("group", "blk"), None),
        P(("group", "blk"), None),
    )
    return jax.shard_map(
        per_device,
        mesh=mesh,
        in_specs=placed,
        out_specs=P(("group", "blk"), None, None, None),
        check_vma=False,
    )
```

```python
import functools

import jax
import jax.numpy as jnp
from jax import lax
from jax.experimental import pallas as pl
from jax.experimental.pallas import tpu as pltpu
from jax.sharding import PartitionSpec as P

MESH = pl.DeviceIdType.MESH
VMEM_LIMIT = 53 * 1024 * 1024


def partner(me, k, n):
    out = 0
    bit = 1
    while bit < n:
        out = out + bit * ((me // bit + k // bit) % 2)
        bit *= 2
    return out


def offset_of(step, n):
    odd = step % 2
    return (1 - odd) * (n // 2 + step // 2) + odd * ((step + 1) // 2)


def kernel(
    n, tables_in, wave, left, right, out,
    tables, tables_v, wpad, left_v, done, recv, sums, item_of, sum_before,
    local_sem, table_sem, left_sem, halo_send, halo_recv, send_sem, recv_sem,
):
    me = lax.axis_index("blk")
    blocks, term_count = left.shape[0], left.shape[1]
    vectors, width = wave.shape[1], wave.shape[2]
    items = blocks * term_count
    per = items // n
    last = n - 1

    barrier = pltpu.get_barrier_semaphore()

    @pl.loop(1, n)
    def _(k):
        pl.semaphore_signal(
            barrier, inc=1, device_id={"blk": partner(me, k, n)}, device_id_type=MESH
        )

    table_copies = [
        pltpu.make_async_copy(source, target, table_sem.at[i])
        for i, (source, target) in enumerate(
            ((tables_in, tables), (tables_in, tables_v))
        )
    ]
    for copy in table_copies:
        copy.start()
    wave_copy = pltpu.make_async_copy(wave, wpad.at[pl.ds(1, blocks)], local_sem.at[0])
    wave_copy.start()
    own = pl.ds(me * per, per)
    own_copy = pltpu.make_async_copy(right.at[own], recv.at[own], local_sem.at[1])
    own_copy.start()
    left_copies = [
        pltpu.make_async_copy(left.at[a], left_v.at[a], left_sem.at[a]) for a in range(blocks)
    ]
    for copy in left_copies:
        copy.start()

    pl.semaphore_wait(barrier, n - 1)

    def halo(up):
        return pltpu.make_async_remote_copy(
            src_ref=wave.at[blocks - 1 if up else 0],
            dst_ref=wpad.at[0 if up else blocks + 1],
            send_sem=halo_send.at[1 if up else 0],
            recv_sem=halo_recv.at[1 if up else 0],
            device_id={"blk": (me + 1) % n if up else (me + n - 1) % n},
            device_id_type=MESH,
        )

    @pl.when(me < last)
    def _():
        halo(True).start()

    @pl.when(me > 0)
    def _():
        halo(False).start()

    def sending(step):
        peer = partner(me, offset_of(step, n), n)
        return pltpu.make_async_remote_copy(
            src_ref=right.at[pl.ds(peer * per, per)],
            dst_ref=recv.at[pl.ds(me * per, per)],
            send_sem=send_sem.at[step],
            recv_sem=recv_sem.at[step],
            device_id={"blk": peer},
            device_id_type=MESH,
        )

    def arriving(step):
        peer = partner(me, offset_of(step, n), n)
        here = recv.at[pl.ds(peer * per, per)]
        return pltpu.make_async_remote_copy(
            src_ref=here,
            dst_ref=here,
            send_sem=send_sem.at[step],
            recv_sem=recv_sem.at[step],
            device_id={"blk": peer},
            device_id_type=MESH,
        )

    @pl.loop(0, n - 1)
    def _(step):
        sending(step).start()

    for copy in table_copies:
        copy.wait()

    table = tables_v[pl.ds(0, blocks)] // 2
    place = lax.broadcasted_iota(jnp.int32, table.shape, 0) * term_count + lax.broadcasted_iota(
        jnp.int32, table.shape, 1
    )
    offset = partner(me, table // per, n)
    rank = jnp.where(
        offset == 0, 0, jnp.where(offset >= n // 2, 2 * offset - n + 1, 2 * offset)
    )
    position = rank * per + table % per

    def look_up(p, latest):
        here = position == p
        row = jnp.max(here.astype(jnp.int32), axis=1, keepdims=True)
        item_of[p] = jnp.max(jnp.where(here, place, 0))
        sum_before[p] = jnp.max(row * latest)
        return jnp.where(row > 0, p + 1, latest)

    latest = lax.fori_loop(0, items, look_up, jnp.zeros((blocks, 1), jnp.int32))
    rows = lax.broadcasted_iota(jnp.int32, (blocks, 1), 0)
    for a in range(blocks):
        sum_before[items + a] = jnp.max(jnp.where(rows == a, latest, 0))
    sums[0] = jnp.zeros(sums.shape[1:], sums.dtype)

    wave_copy.wait()

    @pl.when(me < last)
    def _():
        halo(True).wait_send()
        halo(False).wait_recv()

    @pl.when(me > 0)
    def _():
        halo(False).wait_send()
        halo(True).wait_recv()

    @pl.when(me == 0)
    def _():
        wpad[0] = jnp.zeros(wpad.shape[1:], wpad.dtype)

    @pl.when(me == last)
    def _():
        wpad[blocks + 1] = jnp.zeros(wpad.shape[1:], wpad.dtype)

    for copy in left_copies:
        copy.wait()

    @pl.loop(0, blocks)
    def _(a):
        @pl.loop(0, term_count)
        def _(t):
            row = a + 1 - tables[blocks, t]
            piece = wpad[row]
            beside = jnp.concatenate([piece[v] for v in range(vectors)], axis=1)
            product = jnp.dot(left_v[a, t], beside, preferred_element_type=jnp.float32)
            product = (product * (tables[a, t] % 2).astype(jnp.float32)).astype(jnp.bfloat16)
            for v in range(vectors):
                done[a * term_count + t, pl.ds(v * width, width)] = product[
                    :, v * width : (v + 1) * width
                ]

    def multiply(place, first):
        for j in range(per):
            term = lax.dot_general(
                done[item_of[place + j]],
                recv[first + j],
                (((1,), (1,)), ((), ())),
                preferred_element_type=jnp.float32,
            ).astype(jnp.bfloat16)
            sums[place + j + 1] = sums[sum_before[place + j]] + term.astype(jnp.float32)

    own_copy.wait()
    multiply(0, me * per)
    @pl.loop(0, n - 1)
    def _(step):
        arriving(step).wait_recv()
        multiply((step + 1) * per, partner(me, offset_of(step, n), n) * per)

    @pl.loop(0, blocks)
    def _(a):
        total = sums[sum_before[items + a]]
        for v in range(vectors):
            out[a, v] = total[v * width : (v + 1) * width].astype(out.dtype)

    @pl.loop(0, n - 1)
    def _(step):
        sending(step).wait_send()


def per_device(wavefunction, left_operators, right_operators, shifts, term_mask, slot_table):
    n = lax.axis_size("blk")
    blocks, vectors, width = wavefunction.shape[:3]
    term_count = left_operators.shape[1]
    items = blocks * term_count
    per = items // n
    tables = jnp.concatenate([slot_table * 2 + term_mask, shifts[None]], axis=0)
    hbm = pl.BlockSpec(memory_space=pltpu.HBM)
    dma = pltpu.SemaphoreType.DMA
    return pl.pallas_call(
        functools.partial(kernel, n),
        out_shape=jax.ShapeDtypeStruct(wavefunction.shape, jnp.bfloat16),
        in_specs=[hbm] * 4,
        out_specs=pl.BlockSpec(memory_space=pltpu.VMEM),
        scratch_shapes=[
            pltpu.SMEM(tables.shape, jnp.int32),
            pltpu.VMEM(tables.shape, jnp.int32),
            pltpu.VMEM((blocks + 2, vectors, width, width), jnp.bfloat16),
            pltpu.VMEM((blocks, term_count, width, width), jnp.bfloat16),
            pltpu.VMEM((items, vectors * width, width), jnp.bfloat16),
            pltpu.VMEM((items, width, width), jnp.bfloat16),
            pltpu.VMEM((items + 1, vectors * width, width), jnp.float32),
            pltpu.SMEM((items,), jnp.int32),
            pltpu.SMEM((items + blocks,), jnp.int32),
            dma((2,)),
            dma((2,)),
            dma((blocks,)),
            dma((2,)),
            dma((2,)),
            dma((n - 1,)),
            dma((n - 1,)),
        ],
        compiler_params=pltpu.CompilerParams(
            collective_id=0, has_side_effects=True, vmem_limit_bytes=VMEM_LIMIT
        ),
        cost_estimate=pl.CostEstimate(
            flops=4 * items * vectors * width**3,
            bytes_accessed=4 * items * width * width,
            transcendentals=0,
        ),
        name="sector_product",
    )(tables, wavefunction, left_operators, right_operators)


def solution(mesh):
    placed = (
        P(("group", "blk"), None, None, None),
        P(("group", "blk"), None, None, None),
        P(("group", "blk"), None, None),
        P("group"),
        P(("group", "blk"), None),
        P(("group", "blk"), None),
    )
    return jax.shard_map(
        per_device,
        mesh=mesh,
        in_specs=placed,
        out_specs=P(("group", "blk"), None, None, None),
        check_vma=False,
    )
```

```python
import functools

import jax
import jax.numpy as jnp
from jax import lax
from jax.experimental import pallas as pl
from jax.experimental.pallas import tpu as pltpu
from jax.sharding import PartitionSpec as P

MESH = pl.DeviceIdType.MESH
VMEM_LIMIT = 53 * 1024 * 1024


def partner(me, k, n):
    out = 0
    bit = 1
    while bit < n:
        out = out + bit * ((me // bit + k // bit) % 2)
        bit *= 2
    return out


def offset_of(step, n):
    odd = step % 2
    return (1 - odd) * (n // 2 + step // 2) + odd * ((step + 1) // 2)


def kernel(
    n, tables_in, wave, left, right, out,
    tables, tables_v, wpad, left_v, done, recv, sums, item_of, sum_before,
    local_sem, table_sem, left_sem, halo_send, halo_recv, send_sem, recv_sem,
):
    me = lax.axis_index("blk")
    blocks, term_count = left.shape[0], left.shape[1]
    vectors, width = wave.shape[1], wave.shape[2]
    items = blocks * term_count
    per = items // n
    last = n - 1

    barrier = pltpu.get_barrier_semaphore()

    @pl.loop(1, n)
    def _(k):
        pl.semaphore_signal(
            barrier, inc=1, device_id={"blk": partner(me, k, n)}, device_id_type=MESH
        )

    table_copies = [
        pltpu.make_async_copy(source, target, table_sem.at[i])
        for i, (source, target) in enumerate(
            ((tables_in, tables), (tables_in, tables_v))
        )
    ]
    for copy in table_copies:
        copy.start()
    wave_copy = pltpu.make_async_copy(wave, wpad.at[pl.ds(1, blocks)], local_sem.at[0])
    wave_copy.start()
    own = pl.ds(me * per, per)
    own_copy = pltpu.make_async_copy(right.at[own], recv.at[own], local_sem.at[1])
    own_copy.start()
    left_copies = [
        pltpu.make_async_copy(left.at[a], left_v.at[a], left_sem.at[a]) for a in range(blocks)
    ]

    pl.semaphore_wait(barrier, n - 1)

    def halo(up):
        return pltpu.make_async_remote_copy(
            src_ref=wave.at[blocks - 1 if up else 0],
            dst_ref=wpad.at[0 if up else blocks + 1],
            send_sem=halo_send.at[1 if up else 0],
            recv_sem=halo_recv.at[1 if up else 0],
            device_id={"blk": (me + 1) % n if up else (me + n - 1) % n},
            device_id_type=MESH,
        )

    @pl.when(me < last)
    def _():
        halo(True).start()

    @pl.when(me > 0)
    def _():
        halo(False).start()

    def sending(step):
        peer = partner(me, offset_of(step, n), n)
        return pltpu.make_async_remote_copy(
            src_ref=right.at[pl.ds(peer * per, per)],
            dst_ref=recv.at[pl.ds(me * per, per)],
            send_sem=send_sem.at[step],
            recv_sem=recv_sem.at[step],
            device_id={"blk": peer},
            device_id_type=MESH,
        )

    def arriving(step):
        peer = partner(me, offset_of(step, n), n)
        here = recv.at[pl.ds(peer * per, per)]
        return pltpu.make_async_remote_copy(
            src_ref=here,
            dst_ref=here,
            send_sem=send_sem.at[step],
            recv_sem=recv_sem.at[step],
            device_id={"blk": peer},
            device_id_type=MESH,
        )

    @pl.loop(0, n - 1)
    def _(step):
        sending(step).start()

    for copy in left_copies:
        copy.start()

    for copy in table_copies:
        copy.wait()

    table = tables_v[pl.ds(0, blocks)] // 2
    place = lax.broadcasted_iota(jnp.int32, table.shape, 0) * term_count + lax.broadcasted_iota(
        jnp.int32, table.shape, 1
    )
    offset = partner(me, table // per, n)
    rank = jnp.where(
        offset == 0, 0, jnp.where(offset >= n // 2, 2 * offset - n + 1, 2 * offset)
    )
    position = rank * per + table % per

    def look_up(p, latest):
        here = position == p
        row = jnp.max(here.astype(jnp.int32), axis=1, keepdims=True)
        item_of[p] = jnp.max(jnp.where(here, place, 0))
        sum_before[p] = jnp.max(row * latest)
        return jnp.where(row > 0, p + 1, latest)

    latest = lax.fori_loop(0, items, look_up, jnp.zeros((blocks, 1), jnp.int32))
    rows = lax.broadcasted_iota(jnp.int32, (blocks, 1), 0)
    for a in range(blocks):
        sum_before[items + a] = jnp.max(jnp.where(rows == a, latest, 0))
    sums[0] = jnp.zeros(sums.shape[1:], sums.dtype)

    wave_copy.wait()

    @pl.when(me < last)
    def _():
        halo(True).wait_send()
        halo(False).wait_recv()

    @pl.when(me > 0)
    def _():
        halo(False).wait_send()
        halo(True).wait_recv()

    @pl.when(me == 0)
    def _():
        wpad[0] = jnp.zeros(wpad.shape[1:], wpad.dtype)

    @pl.when(me == last)
    def _():
        wpad[blocks + 1] = jnp.zeros(wpad.shape[1:], wpad.dtype)

    for copy in left_copies:
        copy.wait()

    @pl.loop(0, blocks)
    def _(a):
        @pl.loop(0, term_count)
        def _(t):
            row = a + 1 - tables[blocks, t]
            piece = wpad[row]
            beside = jnp.concatenate([piece[v] for v in range(vectors)], axis=1)
            product = jnp.dot(left_v[a, t], beside, preferred_element_type=jnp.float32)
            product = (product * (tables[a, t] % 2).astype(jnp.float32)).astype(jnp.bfloat16)
            for v in range(vectors):
                done[a * term_count + t, pl.ds(v * width, width)] = product[
                    :, v * width : (v + 1) * width
                ]

    def multiply(place, first):
        for j in range(per):
            term = lax.dot_general(
                done[item_of[place + j]],
                recv[first + j],
                (((1,), (1,)), ((), ())),
                preferred_element_type=jnp.float32,
            ).astype(jnp.bfloat16)
            sums[place + j + 1] = sums[sum_before[place + j]] + term.astype(jnp.float32)

    own_copy.wait()
    multiply(0, me * per)
    @pl.loop(0, n - 1)
    def _(step):
        arriving(step).wait_recv()
        multiply((step + 1) * per, partner(me, offset_of(step, n), n) * per)

    @pl.loop(0, blocks)
    def _(a):
        total = sums[sum_before[items + a]]
        for v in range(vectors):
            out[a, v] = total[v * width : (v + 1) * width].astype(out.dtype)

    @pl.loop(0, n - 1)
    def _(step):
        sending(step).wait_send()


def per_device(wavefunction, left_operators, right_operators, shifts, term_mask, slot_table):
    n = lax.axis_size("blk")
    blocks, vectors, width = wavefunction.shape[:3]
    term_count = left_operators.shape[1]
    items = blocks * term_count
    per = items // n
    tables = jnp.concatenate([slot_table * 2 + term_mask, shifts[None]], axis=0)
    hbm = pl.BlockSpec(memory_space=pltpu.HBM)
    dma = pltpu.SemaphoreType.DMA
    return pl.pallas_call(
        functools.partial(kernel, n),
        out_shape=jax.ShapeDtypeStruct(wavefunction.shape, jnp.bfloat16),
        in_specs=[hbm] * 4,
        out_specs=pl.BlockSpec(memory_space=pltpu.VMEM),
        scratch_shapes=[
            pltpu.SMEM(tables.shape, jnp.int32),
            pltpu.VMEM(tables.shape, jnp.int32),
            pltpu.VMEM((blocks + 2, vectors, width, width), jnp.bfloat16),
            pltpu.VMEM((blocks, term_count, width, width), jnp.bfloat16),
            pltpu.VMEM((items, vectors * width, width), jnp.bfloat16),
            pltpu.VMEM((items, width, width), jnp.bfloat16),
            pltpu.VMEM((items + 1, vectors * width, width), jnp.float32),
            pltpu.SMEM((items,), jnp.int32),
            pltpu.SMEM((items + blocks,), jnp.int32),
            dma((2,)),
            dma((2,)),
            dma((blocks,)),
            dma((2,)),
            dma((2,)),
            dma((n - 1,)),
            dma((n - 1,)),
        ],
        compiler_params=pltpu.CompilerParams(
            collective_id=0, has_side_effects=True, vmem_limit_bytes=VMEM_LIMIT
        ),
        cost_estimate=pl.CostEstimate(
            flops=4 * items * vectors * width**3,
            bytes_accessed=4 * items * width * width,
            transcendentals=0,
        ),
        name="sector_product",
    )(tables, wavefunction, left_operators, right_operators)


def solution(mesh):
    placed = (
        P(("group", "blk"), None, None, None),
        P(("group", "blk"), None, None, None),
        P(("group", "blk"), None, None),
        P("group"),
        P(("group", "blk"), None),
        P(("group", "blk"), None),
    )
    return jax.shard_map(
        per_device,
        mesh=mesh,
        in_specs=placed,
        out_specs=P(("group", "blk"), None, None, None),
        check_vma=False,
    )
```
